32 devices in a mesh: groups: 2 (over x), dev: 8 (over z, y), sub: 2 (over core).
Axes of the slice: x: 2, y: 2, z: 4, core: 2. Of those that a mesh axis runs over, the one named last changes fastest.
Arguments:
- hidden_in: bfloat16 [2, 64, 6144], P(None, ('groups', 'dev', 'sub')), parts along dimension 1, may hold values from -6 to 6
- queries: bfloat16 [2, 64, 6144], P(None, ('groups', 'dev', 'sub')), parts along dimension 1, may hold values from -8 to 8
- key_new: bfloat16 [2, 64, 1024], P(None, ('groups', 'dev', 'sub')), parts along dimension 1, may hold values from -8 to 8
- value_new: bfloat16 [2, 64, 1024], P(None, ('groups', 'dev', 'sub')), parts along dimension 1, may hold values from -6 to 6
- key_cache: bfloat16 [2, 64, 64, 1024], P(None, ('groups', 'dev', 'sub')), parts along dimension 1, may hold values from -8 to 8
- value_cache: bfloat16 [2, 64, 64, 1024], P(None, ('groups', 'dev', 'sub')), parts along dimension 1, may hold values from -6 to 6
- cache_length: int32 [2, 64], P(None, ('groups', 'dev', 'sub')), parts along dimension 1, may hold values from 1 to 64, as said below
- expert_ids: int32 [2, 64, 2], P(None, ('groups', 'dev', 'sub')), parts along dimension 1, may hold values from 0 to 7, as said below
- route_logits: float32 [2, 64, 2], P(None, ('groups', 'dev', 'sub')), parts along dimension 1, may hold values from -6 to 6
- norm_gain: float32 [6144], replicated, may hold values from 0.1 to 1.9
- w_gate: bfloat16 [6144, 16384], P('sub', 'dev'), may hold values from -0.078125 to 0.078125
- w_up: bfloat16 [6144, 16384], P('sub', 'dev'), may hold values from -0.078125 to 0.078125
- w_down: bfloat16 [16384, 6144], P('dev', 'sub'), may hold values from -0.0625 to 0.0625
Outputs:
- layer_out: bfloat16 [2, 64, 6144], P(None, ('groups', 'dev', 'sub')), parts along dimension 1
The draws below stay inside these ranges and needn't reach their ends.
There are 2 independent parts, one for each index of `groups`. The reference program is written for one: setup_inputs(seed, part) draws one part's arguments, and reference() takes and returns one part's arrays. A program takes and returns all parts, laid end to end along the dimension named above; an argument that names none is the same for every part. Nothing has to cross between parts.
Inputs may be any that keep to these rules, and one draw needn't show every extreme that they name: `cache_length`: in each micro-batch some row has exactly 64 filled slots. `expert_ids`: the two ids of a row differ. In each aligned block of 4 rows of a micro-batch (the rows of the devices sharing one index of dev), each expert below 2 is chosen by at most 3 rows and one of them by exactly 3; in some micro-batch one expert below 2 is chosen by 3 rows in every block.
All inputs are finite; a program needn't handle non-finite values.
Results may differ from the reference program's by a relative error of at most 0.005.
Values may be sent and summed in bfloat16 or wider, within the bound.
A program may use at most 128 MiB of HBM per device.

```python
import jax
import jax.numpy as jnp
import numpy as np
from jax import lax

D = 6144
HEADS = 48
KV_HEADS = 8
HEAD_DIM = 128
EXPERTS = 8
EXP_HIDDEN = 8192
EXP_FLIGHT = 2
MB = 2
CTX = 64
ROWS = 32
PAIR_ROWS = 4
CAP = 3


def draw_queries(key, part):
    key = jax.random.fold_in(key, 11)
    array_shape = (MB, ROWS, D)
    values = jnp.clip(jax.random.normal(key, array_shape, jnp.float32), -6.0, 6.0)
    return values.astype(jnp.bfloat16)


def draw_key_cache(key, part):
    key = jax.random.fold_in(key, 13)
    array_shape = (MB, ROWS, CTX, KV_HEADS * HEAD_DIM)
    values = jnp.clip(jax.random.normal(key, array_shape, jnp.float32), -6.0, 6.0)
    return values.astype(jnp.bfloat16)


def draw_key_new(key, part):
    key = jax.random.fold_in(key, 17)
    array_shape = (MB, ROWS, KV_HEADS * HEAD_DIM)
    values = jnp.clip(jax.random.normal(key, array_shape, jnp.float32), -6.0, 6.0)
    return values.astype(jnp.bfloat16)


def draw_cache_length(key, part):
    key = jax.random.fold_in(key, 19)
    length_key, place_key = jax.random.split(key)
    lengths = jax.random.randint(length_key, (MB, ROWS), 1, CTX + 1)
    longest = jax.random.randint(place_key, (MB, 1), 0, ROWS)
    row_index = jnp.arange(ROWS, dtype=jnp.int32)[None, :]
    return jnp.where(row_index == longest, CTX, lengths).astype(jnp.int32)


def draw_expert_ids(key, part):
    key = jax.random.fold_in(key, 23)
    blocks = ROWS // PAIR_ROWS
    remaining = 2 * PAIR_ROWS - CAP
    base_load = remaining // (EXPERTS - 1)
    surplus = remaining % (EXPERTS - 1)
    block_loads = [CAP] + [base_load + 1] * surplus + [base_load] * (EXPERTS - 1 - surplus)
    position_owner = jnp.asarray(np.repeat(np.arange(EXPERTS), block_loads), jnp.int32)
    shared = jax.random.randint(jax.random.fold_in(key, 1), (), 0, EXP_FLIGHT)
    block_keys = jax.random.split(jax.random.fold_in(key, 2), MB * blocks)

    def one_block(sub_key, block_number):
        hot_key, perm_key, row_key, swap_key = jax.random.split(sub_key, 4)
        own_hot = jax.random.randint(hot_key, (), 0, EXP_FLIGHT)
        hot_expert = jnp.where(block_number < blocks, shared, own_hot).astype(jnp.int32)
        others = (hot_expert + 1 + jax.random.permutation(perm_key, EXPERTS - 1).astype(jnp.int32)) % EXPERTS
        expert_order = jnp.concatenate([hot_expert[None], others])
        placed = expert_order[position_owner]
        shuffle = jax.random.permutation(row_key, PAIR_ROWS)
        leading = placed[:PAIR_ROWS][shuffle]
        trailing = placed[PAIR_ROWS:][shuffle]
        swapped = jax.random.randint(swap_key, (PAIR_ROWS,), 0, 2) == 1
        return jnp.stack([jnp.where(swapped, trailing, leading), jnp.where(swapped, leading, trailing)], axis=1)
    chosen_ids = jax.vmap(one_block)(block_keys, jnp.arange(MB * blocks, dtype=jnp.int32))
    return chosen_ids.reshape(MB, ROWS, 2).astype(jnp.int32)


def steps_of(rng, dims, cuts, least, high):
    def one(dim, parts):
        draws = jax.random.uniform(jax.random.fold_in(jax.random.fold_in(rng, 6), dim), (parts,), jnp.float32, least / len(cuts), high / len(cuts))
        return jnp.repeat(jnp.exp(draws), dims[dim] // parts).reshape((-1,) + (1,) * (len(dims) - dim - 1))

    gain = one(*cuts[0])
    for cut in cuts[1:]:
        gain = gain * one(*cut)
    return gain


def normal_values(key, extent, scale, bound, cuts=(), held_as=jnp.bfloat16):
    result = scale * jax.random.normal(key, extent, jnp.float32)
    if cuts:
        result = result * steps_of(key, extent, cuts, -0.22, 0.18)
    return jnp.clip(result, -bound, bound).astype(held_as)


def setup_inputs(seed: int = 0, part: int = 0) -> dict:
    key_of = jax.random.split(jax.random.key(seed), 14)
    part_splits = jax.random.split(jax.random.fold_in(key_of[13], part), 14)
    hidden_in = normal_values(part_splits[0], (MB, ROWS, D), 1.0, 6.0, ((1, 16),))
    queries = draw_queries(jax.random.fold_in(jax.random.fold_in(key_of[13], part), 71), part)
    key_new = draw_key_new(jax.random.fold_in(jax.random.fold_in(key_of[13], part), 71), part)
    value_new = normal_values(part_splits[3], (MB, ROWS, KV_HEADS * HEAD_DIM), 1.0, 6.0, ((1, 16),))
    key_cache = draw_key_cache(jax.random.fold_in(jax.random.fold_in(key_of[13], part), 71), part)
    value_cache = normal_values(part_splits[5], (MB, ROWS, CTX, KV_HEADS * HEAD_DIM), 1.0, 6.0, ((1, 16),))
    cache_length = draw_cache_length(jax.random.fold_in(jax.random.fold_in(key_of[13], part), 71), part)
    expert_ids = draw_expert_ids(jax.random.fold_in(jax.random.fold_in(key_of[13], part), 71), part)
    route_logits = normal_values(part_splits[8], (MB, ROWS, 2), 1.5, 6.0, ((1, 16),), jnp.float32)
    norm_gain = jnp.clip(1.0 + 0.18 * jax.random.normal(key_of[9], (D,), jnp.float32), 0.1, 1.9)
    w_gate = normal_values(key_of[10], (D, EXP_FLIGHT * EXP_HIDDEN), D ** -0.5, 0.078125, ((0, 2), (1, 8)))
    w_up = normal_values(key_of[11], (D, EXP_FLIGHT * EXP_HIDDEN), D ** -0.5, 0.078125, ((0, 2), (1, 8)))
    w_down = normal_values(key_of[12], (EXP_FLIGHT * EXP_HIDDEN, D), EXP_HIDDEN ** -0.5, 0.0625, ((0, 8), (1, 2)))
    return {"hidden_in": hidden_in, "queries": queries, "key_new": key_new, "value_new": value_new, "key_cache": key_cache, "value_cache": value_cache, "cache_length": cache_length, "expert_ids": expert_ids, "route_logits": route_logits, "norm_gain": norm_gain, "w_gate": w_gate, "w_up": w_up, "w_down": w_down}


masked_score = -1e+30

def attend(queries, key_new, value_new, key_cache, value_cache, lengths):
    row_count = queries.shape[0]
    groups = HEADS // KV_HEADS
    inv_root = 1.0 / HEAD_DIM ** 0.5
    query_heads = queries.astype(jnp.float32).reshape(row_count, KV_HEADS, groups, HEAD_DIM)
    cache_keys = key_cache.astype(jnp.float32).reshape(row_count, CTX, KV_HEADS, HEAD_DIM)
    cache_values = value_cache.astype(jnp.float32).reshape(row_count, CTX, KV_HEADS, HEAD_DIM)
    fresh_keys = key_new.astype(jnp.float32).reshape(row_count, KV_HEADS, HEAD_DIM)
    fresh_values = value_new.astype(jnp.float32).reshape(row_count, KV_HEADS, HEAD_DIM)
    cache_scores = jnp.einsum('rkgd,rjkd->rkgj', query_heads, cache_keys) * inv_root
    fresh_scores = jnp.einsum('rkgd,rkd->rkg', query_heads, fresh_keys) * inv_root
    visible = jnp.arange(CTX, dtype=jnp.int32)[None, :] < lengths[:, None]
    visible = visible[:, None, None, :]
    cache_scores = jnp.where(visible, cache_scores, masked_score)
    row_max = jnp.maximum(lax.optimization_barrier(jnp.max(cache_scores, axis=-1)), fresh_scores)
    cache_exp = jnp.where(visible, jnp.exp(cache_scores - row_max[..., None]), 0.0)
    fresh_exp = jnp.exp(fresh_scores - row_max)
    denominator = lax.optimization_barrier(jnp.sum(cache_exp, axis=-1)) + fresh_exp
    cache_probs = (cache_exp / denominator[..., None]).astype(jnp.bfloat16)
    fresh_probs = (fresh_exp / denominator).astype(jnp.bfloat16)
    context = jnp.einsum('rkgj,rjkd->rkgd', cache_probs.astype(jnp.float32), cache_values)
    context = context + fresh_probs.astype(jnp.float32)[..., None] * fresh_values[:, :, None, :]
    return context.reshape(row_count, HEADS * HEAD_DIM)

def route_table(chosen_ids, logits):
    spread = logits[:, 0].astype(jnp.float32) - logits[:, 1].astype(jnp.float32)
    gates = jax.nn.sigmoid(jnp.stack([spread, -spread], axis=1))
    expert_range = jnp.arange(EXP_FLIGHT, dtype=jnp.int32)
    hits = (chosen_ids[:, :, None] == expert_range[None, None, :]).astype(gates.dtype)
    routed = lax.optimization_barrier(jnp.sum(hits, axis=1))
    weight = lax.optimization_barrier(jnp.sum(hits * gates[:, :, None], axis=1))
    return jnp.stack([routed, weight], axis=2)

def select_slots(routing, capacity):
    routed = routing[..., 0]
    position = jnp.cumsum(routed, axis=1) - routed
    places = jnp.arange(capacity, dtype=jnp.int32).astype(routing.dtype)
    selector = routed[..., None] * (position[..., None] == places).astype(routing.dtype)
    return jnp.transpose(selector, (0, 2, 3, 1))

def reference(hidden_in, queries, key_new, value_new, key_cache, value_cache, cache_length, expert_ids, route_logits, norm_gain, w_gate, w_up, w_down):
    blocks = ROWS // PAIR_ROWS
    results = []
    for micro_step in range(MB):
        context = attend(queries[micro_step], key_new[micro_step], value_new[micro_step], key_cache[micro_step], value_cache[micro_step], cache_length[micro_step])
        resid = hidden_in[micro_step].astype(jnp.float32) + context
        inv_rms = lax.rsqrt(lax.optimization_barrier(jnp.mean(resid * resid, axis=1, keepdims=True)) + 1e-05)
        normed = (resid * inv_rms * norm_gain[None, :]).astype(jnp.bfloat16)
        routing = route_table(expert_ids[micro_step], route_logits[micro_step]).reshape(blocks, PAIR_ROWS, EXP_FLIGHT, 2)
        selector = select_slots(routing, CAP)
        block_rows = normed.reshape(blocks, PAIR_ROWS, D).astype(jnp.float32)
        mixture = jnp.zeros((blocks, PAIR_ROWS, D), jnp.float32)
        for expert in range(EXP_FLIGHT):
            picked = jnp.einsum('bcp,bpd->bcd', selector[:, expert], block_rows).astype(jnp.bfloat16)
            slot_matrix = picked.reshape(blocks * CAP, D)
            lower = expert * EXP_HIDDEN
            upper = lower + EXP_HIDDEN
            gate_sum = jnp.dot(slot_matrix, w_gate[:, lower:upper], preferred_element_type=jnp.float32)
            up_sum = jnp.dot(slot_matrix, w_up[:, lower:upper], preferred_element_type=jnp.float32)
            hidden_units = (jax.nn.silu(gate_sum) * up_sum).astype(jnp.bfloat16)
            expert_out = jnp.dot(hidden_units, w_down[lower:upper, :], preferred_element_type=jnp.float32).reshape(blocks, CAP, D)
            weights = selector[:, expert] * routing[:, :, expert, 1][:, None, :]
            mixture = mixture + jnp.einsum('bcp,bcd->bpd', weights, expert_out, precision=lax.Precision.HIGHEST)
        results.append((resid + mixture.reshape(ROWS, D)).astype(jnp.bfloat16))
    return jnp.stack(results, axis=0)
```

```python
import functools

import jax
import jax.numpy as jnp
from jax import lax
from jax.experimental import pallas as pl
from jax.experimental.pallas import tpu as pltpu
from jax.sharding import PartitionSpec as P

HEADS = 48
KV_HEADS = 8
HEAD_DIM = 128
GROUP = HEADS // KV_HEADS
EXP_FLIGHT = 2
PIECES = 4
RETURN_CHUNKS = 3

masked_score = -1e30
f32 = jnp.float32
bf16 = jnp.bfloat16


def permutation(senders, rows, inverse):
    size = senders * PIECES * rows
    i = lax.broadcasted_iota(jnp.int32, (size, size), 0)
    c = lax.broadcasted_iota(jnp.int32, (size, size), 1)
    if inverse:
        i, c = c, i
    row_bits = rows.bit_length() - 1
    sender_bits = senders.bit_length() - 1
    row = i & (rows - 1)
    sender = lax.shift_right_logical(i, row_bits) & (senders - 1)
    piece = lax.shift_right_logical(i, row_bits + sender_bits)
    at = sender * (PIECES * rows) + piece * rows + row
    return jnp.where(at == c, 1.0, 0.0).astype(f32).astype(bf16)


def layer_kernel(
    micro, own, dev_count, sub_count, chunk,
    hidden_ref, query_ref, knew_ref, vnew_ref, kcache_ref, vcache_ref, length_ref,
    ids_ref, logit_ref, gain_ref, wg_ref, wu_ref, wd_ref,
    out_ref,
    kbuf, vbuf, wg, wu, wd, qbig, ctx, resid, send, arrived, perm, perm_back,
    x, parts, other, units, acc, back, returned, result,
    kv_sem, wg_sem, wu_sem, wd_sem, send_sem, arrive_sem, part_sem, other_sem, back_sem, return_sem,
):
    rows = micro * own
    count = dev_count * sub_count
    my_dev = lax.axis_index("dev")
    my_sub = lax.axis_index("sub")
    me = my_dev * sub_count + my_sub
    half = wg.shape[1]
    piece = half // PIECES
    chunks = wg.shape[0]
    width = half // RETURN_CHUNKS
    small = width // PIECES
    group_width = GROUP * HEAD_DIM

    kv_copies = [
        pltpu.make_async_copy(kcache_ref, kbuf, kv_sem.at[0]),
        pltpu.make_async_copy(vcache_ref, vbuf, kv_sem.at[1]),
    ]
    for copy in kv_copies:
        copy.start()

    def wg_copy(n):
        cols = pl.ds(pl.multiple_of(n * chunk, chunk), chunk)
        return (
            pltpu.make_async_copy(wg_ref.at[:, cols], wg.at[n], wg_sem.at[n]),
            pltpu.make_async_copy(wu_ref.at[:, cols], wu.at[n], wu_sem.at[n]),
        )

    def wd_copy(n):
        return pltpu.make_async_copy(wd_ref.at[pl.ds(n * chunk, chunk)], wd.at[n], wd_sem.at[n])

    for n in range(chunks):
        for copy in wg_copy(n):
            copy.start()
    for n in range(chunks):
        wd_copy(n).start()

    def peer(offset):
        target = lax.rem(me + offset, count)
        return target, {"dev": target // sub_count, "sub": lax.rem(target, sub_count)}

    barrier = pltpu.get_barrier_semaphore()
    for offset in range(1, count):
        pl.semaphore_signal(
            barrier, inc=1, device_id=peer(offset)[1], device_id_type=pl.DeviceIdType.MESH
        )

    perm[...] = permutation(count, rows, False)
    perm_back[...] = permutation(count, rows, True)

    inv_root = 1.0 / HEAD_DIM**0.5
    qbig[...] = jnp.zeros_like(qbig)
    for r in range(rows):
        m, i = divmod(r, own)
        q = query_ref[m].astype(f32)
        for h in range(HEADS):
            k = h // GROUP
            qbig[r, h : h + 1, k * HEAD_DIM : (k + 1) * HEAD_DIM] = q[
                i : i + 1, h * HEAD_DIM : (h + 1) * HEAD_DIM
            ]
    for copy in kv_copies:
        copy.wait()
    slot = lax.broadcasted_iota(jnp.int32, (HEADS, kbuf.shape[2]), 1)
    for r in range(rows):
        m, i = divmod(r, own)
        q = qbig[r]
        scores = lax.dot_general(
            q.astype(bf16), kbuf[m, i], (((1,), (1,)), ((), ())), preferred_element_type=f32
        ) * inv_root
        new_key = knew_ref[m].astype(f32)[i : i + 1]
        new_value = vnew_ref[m].astype(f32)[i : i + 1]
        fresh = jnp.sum(q * new_key, axis=1, keepdims=True) * inv_root
        visible = slot < length_ref[m, i]
        scores = jnp.where(visible, scores, masked_score)
        top = jnp.maximum(jnp.max(scores, axis=1, keepdims=True), fresh)
        exps = jnp.where(visible, jnp.exp(scores - top), 0.0)
        fresh_exp = jnp.exp(fresh - top)
        total = jnp.sum(exps, axis=1, keepdims=True) + fresh_exp
        probs = (exps / total).astype(bf16)
        fresh_probs = (fresh_exp / total).astype(bf16).astype(f32)
        wide = jnp.dot(probs, vbuf[m, i], preferred_element_type=f32) + fresh_probs * new_value
        for h in range(HEADS):
            k, g = divmod(h, GROUP)
            ctx[k * rows + r : k * rows + r + 1, g * HEAD_DIM : (g + 1) * HEAD_DIM] = wide[
                h : h + 1, k * HEAD_DIM : (k + 1) * HEAD_DIM
            ]

    squares = jnp.zeros((rows, 1), f32)
    for k in range(KV_HEADS):
        cols = slice(k * group_width, (k + 1) * group_width)
        for m in range(micro):
            base = k * rows + m * own
            resid[m * own : (m + 1) * own, cols] = (
                hidden_ref[m, :, cols].astype(f32) + ctx[base : base + own, :]
            )
        value = resid[:, cols]
        squares = squares + jnp.sum(value * value, axis=1, keepdims=True)
    inv_rms = lax.rsqrt(squares / (KV_HEADS * group_width) + 1e-05)
    for k in range(KV_HEADS):
        cols = slice(k * group_width, (k + 1) * group_width)
        ctx[k * rows : (k + 1) * rows, :] = resid[:, cols] * inv_rms * gain_ref[:, cols]
    for s in range(sub_count):
        send[s] = ctx[s * PIECES * rows : (s + 1) * PIECES * rows, :].astype(bf16)

    pl.semaphore_wait(barrier, count - 1)

    def dispatch(offset):
        target, place = peer(offset)
        return pltpu.make_async_remote_copy(
            src_ref=send.at[lax.rem(target, sub_count)],
            dst_ref=arrived.at[me],
            send_sem=send_sem.at[offset],
            recv_sem=arrive_sem.at[offset],
            device_id=place,
            device_id_type=pl.DeviceIdType.MESH,
        )

    for offset in range(1, count):
        dispatch(offset).start()
    arrived[me] = send[my_sub]
    for offset in range(1, count):
        dispatch(offset).wait_recv()

    grid = arrived[...].reshape(count * PIECES * rows, piece)
    sorted_rows = jnp.dot(perm[...], grid, preferred_element_type=f32).astype(bf16)
    tall = count * rows
    for j in range(PIECES):
        x[:, j * piece : (j + 1) * piece] = sorted_rows[j * tall : (j + 1) * tall]

    def exchange(n):
        return pltpu.make_async_remote_copy(
            src_ref=parts.at[n],
            dst_ref=other.at[n],
            send_sem=part_sem.at[n],
            recv_sem=other_sem.at[n],
            device_id={"dev": my_dev, "sub": 1 - my_sub},
            device_id_type=pl.DeviceIdType.MESH,
        )

    def finish(n):
        exchange(n).wait_recv()
        gate = parts[n, 0] + other[n, 0]
        up = parts[n, 1] + other[n, 1]
        units[n] = (jax.nn.silu(gate) * up).astype(bf16)

    def gate_up(n, carry):
        for copy in wg_copy(n):
            copy.wait()
        parts[n, 0] = jnp.dot(x[...], wg[n], preferred_element_type=f32)
        parts[n, 1] = jnp.dot(x[...], wu[n], preferred_element_type=f32)
        exchange(n).start()

        @pl.when(n > 0)
        def _():
            finish(n - 1)

        return carry

    lax.fori_loop(0, chunks, gate_up, 0)

    for n in range(chunks):
        wd_copy(n).wait()

    def down(c, carry):
        cols = pl.ds(pl.multiple_of(c * width, width), width)
        total = jnp.zeros((tall, width), f32)
        for n in range(chunks - 1):
            total = total + jnp.dot(units[n], wd[n, :, cols], preferred_element_type=f32)
        acc[c] = total
        return carry

    if chunks > 1:
        lax.fori_loop(0, RETURN_CHUNKS, down, 0)
    finish(chunks - 1)

    def give_back(c, offset):
        target, place = peer(offset)
        return pltpu.make_async_remote_copy(
            src_ref=back.at[c, target],
            dst_ref=returned.at[c, me],
            send_sem=back_sem.at[c, offset],
            recv_sem=return_sem.at[c, offset],
            device_id=place,
            device_id_type=pl.DeviceIdType.MESH,
        )

    def last(c, carry):
        cols = pl.ds(pl.multiple_of(c * width, width), width)
        total = jnp.dot(units[chunks - 1], wd[chunks - 1, :, cols], preferred_element_type=f32)
        if chunks > 1:
            total = total + acc[c]
        total = total.astype(bf16)
        stacked = jnp.concatenate(
            [total[:, j * small : (j + 1) * small] for j in range(PIECES)], axis=0
        )
        sorted_out = jnp.dot(perm_back[...], stacked, preferred_element_type=f32).astype(bf16)
        back[c] = sorted_out.reshape(count, PIECES * rows, small)
        for offset in range(1, count):
            give_back(c, offset).start()
        returned[c, me] = back[c, me]
        return carry

    lax.fori_loop(0, RETURN_CHUNKS, last, 0)

    row_at = lax.broadcasted_iota(jnp.int32, (PIECES * rows, HEAD_DIM), 0) & (rows - 1)
    spread = jnp.zeros(row_at.shape, f32)
    first = jnp.full(row_at.shape, -1, jnp.int32)
    second = jnp.full(row_at.shape, -1, jnp.int32)
    for r in range(rows):
        m, i = divmod(r, own)
        spread = jnp.where(row_at == r, logit_ref[m, i, 0] - logit_ref[m, i, 1], spread)
        first = jnp.where(row_at == r, ids_ref[m, i, 0], first)
        second = jnp.where(row_at == r, ids_ref[m, i, 1], second)
    gate_first = jax.nn.sigmoid(spread)
    gate_second = jax.nn.sigmoid(-spread)
    weights = []
    for e in range(EXP_FLIGHT):
        weight = jnp.where(first == e, gate_first, 0.0) + jnp.where(second == e, gate_second, 0.0)
        weights.append(weight[:, :1])

    per_expert = dev_count // EXP_FLIGHT
    for c in range(RETURN_CHUNKS):
        for offset in range(1, count):
            give_back(c, offset).wait_recv()
        for s in range(sub_count):
            mixture = jnp.zeros((PIECES * rows, small), f32)
            for e in range(EXP_FLIGHT):
                expert_sum = jnp.zeros((PIECES * rows, small), f32)
                for b in range(e * per_expert, (e + 1) * per_expert):
                    expert_sum = expert_sum + returned[c, b * sub_count + s].astype(f32)
                mixture = mixture + weights[e] * expert_sum
            for j in range(PIECES):
                start = s * half + c * width + j * small
                cols = slice(start, start + small)
                result[:, cols] = resid[:, cols] + mixture[j * rows : (j + 1) * rows, :]
    for m in range(micro):
        out_ref[m] = result[m * own : (m + 1) * own, :].astype(bf16)

    for offset in range(1, count):
        dispatch(offset).wait_send()
    for n in range(chunks):
        exchange(n).wait_send()
    for c in range(RETURN_CHUNKS):
        for offset in range(1, count):
            give_back(c, offset).wait_send()


def shards(
    hidden_in, queries, key_new, value_new, key_cache, value_cache, cache_length,
    expert_ids, route_logits, norm_gain, w_gate, w_up, w_down,
):
    micro, own, model = hidden_in.shape
    slots = key_cache.shape[2]
    kv_width = key_cache.shape[3]
    dev_count = lax.axis_size("dev")
    sub_count = lax.axis_size("sub")
    count = dev_count * sub_count
    rows = micro * own
    tall = count * rows
    half, hidden = w_gate.shape
    chunk = min(512, hidden)
    chunks = hidden // chunk
    piece = half // PIECES
    width = half // RETURN_CHUNKS
    small = width // PIECES
    lane_rows = PIECES * rows
    vmem = pl.BlockSpec(memory_space=pltpu.VMEM)
    smem = pl.BlockSpec(memory_space=pltpu.SMEM)
    anywhere = pl.BlockSpec(memory_space=pl.ANY)
    dma = pltpu.SemaphoreType.DMA
    return pl.pallas_call(
        functools.partial(layer_kernel, micro, own, dev_count, sub_count, chunk),
        out_shape=jax.ShapeDtypeStruct((micro, own, model), bf16),
        in_specs=[
            vmem, vmem, vmem, vmem, anywhere, anywhere, smem, smem, smem, vmem,
            anywhere, anywhere, anywhere,
        ],
        out_specs=vmem,
        scratch_shapes=[
            pltpu.VMEM((micro, own, slots, kv_width), bf16),
            pltpu.VMEM((micro, own, slots, kv_width), bf16),
            pltpu.VMEM((chunks, half, chunk), bf16),
            pltpu.VMEM((chunks, half, chunk), bf16),
            pltpu.VMEM((chunks, chunk, half), bf16),
            pltpu.VMEM((rows, HEADS, kv_width), f32),
            pltpu.VMEM((KV_HEADS * rows, GROUP * HEAD_DIM), f32),
            pltpu.VMEM((rows, model), f32),
            pltpu.VMEM((sub_count, lane_rows, piece), bf16),
            pltpu.VMEM((count, lane_rows, piece), bf16),
            pltpu.VMEM((count * lane_rows, count * lane_rows), bf16),
            pltpu.VMEM((count * lane_rows, count * lane_rows), bf16),
            pltpu.VMEM((tall, half), bf16),
            pltpu.VMEM((chunks, 2, tall, chunk), f32),
            pltpu.VMEM((chunks, 2, tall, chunk), f32),
            pltpu.VMEM((chunks, tall, chunk), bf16),
            pltpu.VMEM((RETURN_CHUNKS, tall, width), f32),
            pltpu.VMEM((RETURN_CHUNKS, count, lane_rows, small), bf16),
            pltpu.VMEM((RETURN_CHUNKS, count, lane_rows, small), bf16),
            pltpu.VMEM((rows, model), f32),
            dma((2,)),
            dma((chunks,)),
            dma((chunks,)),
            dma((chunks,)),
            dma((count,)),
            dma((count,)),
            dma((chunks,)),
            dma((chunks,)),
            dma((RETURN_CHUNKS, count)),
            dma((RETURN_CHUNKS, count)),
        ],
        compiler_params=pltpu.CompilerParams(
            collective_id=0, has_side_effects=True, vmem_limit_bytes=56 * 2**20
        ),
    )(
        hidden_in, queries, key_new, value_new, key_cache, value_cache, cache_length,
        expert_ids, route_logits, norm_gain.reshape(1, model), w_gate, w_up, w_down,
    )


def solution(mesh):
    return jax.shard_map(
        shards,
        mesh=mesh,
        in_specs=(
            P(None, ("groups", "dev", "sub"), None),
            P(None, ("groups", "dev", "sub"), None),
            P(None, ("groups", "dev", "sub"), None),
            P(None, ("groups", "dev", "sub"), None),
            P(None, ("groups", "dev", "sub"), None, None),
            P(None, ("groups", "dev", "sub"), None, None),
            P(None, ("groups", "dev", "sub")),
            P(None, ("groups", "dev", "sub"), None),
            P(None, ("groups", "dev", "sub"), None),
            P(),
            P("sub", "dev"),
            P("sub", "dev"),
            P("dev", "sub"),
        ),
        out_specs=P(None, ("groups", "dev", "sub"), None),
        check_vma=False,
    )
```

```python
import functools

import jax
import jax.numpy as jnp
from jax import lax
from jax.experimental import pallas as pl
from jax.experimental.pallas import tpu as pltpu
from jax.sharding import PartitionSpec as P

HEADS = 48
KV_HEADS = 8
HEAD_DIM = 128
GROUP = HEADS // KV_HEADS
EXP_FLIGHT = 2
PIECES = 4
RETURN_CHUNKS = 3

masked_score = -1e30
f32 = jnp.float32
bf16 = jnp.bfloat16


def permutation(senders, rows, inverse):
    size = senders * PIECES * rows
    i = lax.broadcasted_iota(jnp.int32, (size, size), 0)
    c = lax.broadcasted_iota(jnp.int32, (size, size), 1)
    if inverse:
        i, c = c, i
    row_bits = rows.bit_length() - 1
    sender_bits = senders.bit_length() - 1
    row = i & (rows - 1)
    sender = lax.shift_right_logical(i, row_bits) & (senders - 1)
    piece = lax.shift_right_logical(i, row_bits + sender_bits)
    at = sender * (PIECES * rows) + piece * rows + row
    return jnp.where(at == c, 1.0, 0.0).astype(f32).astype(bf16)


def layer_kernel(
    micro, own, dev_count, sub_count, chunk,
    hidden_ref, query_ref, knew_ref, vnew_ref, kcache_ref, vcache_ref, length_ref,
    ids_ref, logit_ref, gain_ref, wg_ref, wu_ref, wd_ref,
    out_ref,
    kbuf, vbuf, wg, wu, wd, qbig, ctx, resid, send, arrived, perm, perm_back,
    x, parts, other, units, acc, back, returned, result,
    kv_sem, wg_sem, wu_sem, wd_sem, send_sem, arrive_sem, part_sem, other_sem, back_sem, return_sem,
):
    rows = micro * own
    count = dev_count * sub_count
    my_dev = lax.axis_index("dev")
    my_sub = lax.axis_index("sub")
    me = my_dev * sub_count + my_sub
    half = wg.shape[1]
    piece = half // PIECES
    chunks = wg.shape[0]
    width = half // RETURN_CHUNKS
    small = width // PIECES
    group_width = GROUP * HEAD_DIM

    kv_copies = [
        pltpu.make_async_copy(kcache_ref, kbuf, kv_sem.at[0]),
        pltpu.make_async_copy(vcache_ref, vbuf, kv_sem.at[1]),
    ]
    for copy in kv_copies:
        copy.start()

    def wg_copy(n):
        cols = pl.ds(pl.multiple_of(n * chunk, chunk), chunk)
        return (
            pltpu.make_async_copy(wg_ref.at[:, cols], wg.at[n], wg_sem.at[n]),
            pltpu.make_async_copy(wu_ref.at[:, cols], wu.at[n], wu_sem.at[n]),
        )

    def wd_copy(n):
        return pltpu.make_async_copy(wd_ref.at[pl.ds(n * chunk, chunk)], wd.at[n], wd_sem.at[n])

    for n in range(chunks):
        for copy in wg_copy(n):
            copy.start(priority=1)
    for n in range(chunks):
        wd_copy(n).start(priority=1)

    def peer(offset):
        target = lax.rem(me + offset, count)
        return target, {"dev": target // sub_count, "sub": lax.rem(target, sub_count)}

    barrier = pltpu.get_barrier_semaphore()
    for offset in range(1, count):
        pl.semaphore_signal(
            barrier, inc=1, device_id=peer(offset)[1], device_id_type=pl.DeviceIdType.MESH
        )

    perm[...] = permutation(count, rows, False)
    perm_back[...] = permutation(count, rows, True)

    inv_root = 1.0 / HEAD_DIM**0.5
    qbig[...] = jnp.zeros_like(qbig)
    for r in range(rows):
        m, i = divmod(r, own)
        q = query_ref[m].astype(f32)
        for h in range(HEADS):
            k = h // GROUP
            qbig[r, h : h + 1, k * HEAD_DIM : (k + 1) * HEAD_DIM] = q[
                i : i + 1, h * HEAD_DIM : (h + 1) * HEAD_DIM
            ]
    for copy in kv_copies:
        copy.wait()
    slot = lax.broadcasted_iota(jnp.int32, (HEADS, kbuf.shape[2]), 1)
    for r in range(rows):
        m, i = divmod(r, own)
        q = qbig[r]
        scores = lax.dot_general(
            q.astype(bf16), kbuf[m, i], (((1,), (1,)), ((), ())), preferred_element_type=f32
        ) * inv_root
        new_key = knew_ref[m].astype(f32)[i : i + 1]
        new_value = vnew_ref[m].astype(f32)[i : i + 1]
        fresh = jnp.sum(q * new_key, axis=1, keepdims=True) * inv_root
        visible = slot < length_ref[m, i]
        scores = jnp.where(visible, scores, masked_score)
        top = jnp.maximum(jnp.max(scores, axis=1, keepdims=True), fresh)
        exps = jnp.where(visible, jnp.exp(scores - top), 0.0)
        fresh_exp = jnp.exp(fresh - top)
        total = jnp.sum(exps, axis=1, keepdims=True) + fresh_exp
        probs = (exps / total).astype(bf16)
        fresh_probs = (fresh_exp / total).astype(bf16).astype(f32)
        wide = jnp.dot(probs, vbuf[m, i], preferred_element_type=f32) + fresh_probs * new_value
        for h in range(HEADS):
            k, g = divmod(h, GROUP)
            ctx[k * rows + r : k * rows + r + 1, g * HEAD_DIM : (g + 1) * HEAD_DIM] = wide[
                h : h + 1, k * HEAD_DIM : (k + 1) * HEAD_DIM
            ]

    squares = jnp.zeros((rows, 1), f32)
    for k in range(KV_HEADS):
        cols = slice(k * group_width, (k + 1) * group_width)
        for m in range(micro):
            base = k * rows + m * own
            resid[m * own : (m + 1) * own, cols] = (
                hidden_ref[m, :, cols].astype(f32) + ctx[base : base + own, :]
            )
        value = resid[:, cols]
        squares = squares + jnp.sum(value * value, axis=1, keepdims=True)
    inv_rms = lax.rsqrt(squares / (KV_HEADS * group_width) + 1e-05)
    for k in range(KV_HEADS):
        cols = slice(k * group_width, (k + 1) * group_width)
        ctx[k * rows : (k + 1) * rows, :] = resid[:, cols] * inv_rms * gain_ref[:, cols]
    for s in range(sub_count):
        send[s] = ctx[s * PIECES * rows : (s + 1) * PIECES * rows, :].astype(bf16)

    pl.semaphore_wait(barrier, count - 1)

    def dispatch(offset):
        target, place = peer(offset)
        return pltpu.make_async_remote_copy(
            src_ref=send.at[lax.rem(target, sub_count)],
            dst_ref=arrived.at[me],
            send_sem=send_sem.at[offset],
            recv_sem=arrive_sem.at[offset],
            device_id=place,
            device_id_type=pl.DeviceIdType.MESH,
        )

    for offset in range(1, count):
        dispatch(offset).start()
    arrived[me] = send[my_sub]
    for offset in range(1, count):
        dispatch(offset).wait_recv()

    grid = arrived[...].reshape(count * PIECES * rows, piece)
    sorted_rows = jnp.dot(perm[...], grid, preferred_element_type=f32).astype(bf16)
    tall = count * rows
    for j in range(PIECES):
        x[:, j * piece : (j + 1) * piece] = sorted_rows[j * tall : (j + 1) * tall]

    def exchange(n):
        return pltpu.make_async_remote_copy(
            src_ref=parts.at[n],
            dst_ref=other.at[n],
            send_sem=part_sem.at[n],
            recv_sem=other_sem.at[n],
            device_id={"dev": my_dev, "sub": 1 - my_sub},
            device_id_type=pl.DeviceIdType.MESH,
        )

    def finish(n):
        exchange(n).wait_recv()
        gate = parts[n, 0] + other[n, 0]
        up = parts[n, 1] + other[n, 1]
        units[n] = (jax.nn.silu(gate) * up).astype(bf16)

    def gate_up(n, carry):
        for copy in wg_copy(n):
            copy.wait()
        parts[n, 0] = jnp.dot(x[...], wg[n], preferred_element_type=f32)
        parts[n, 1] = jnp.dot(x[...], wu[n], preferred_element_type=f32)
        exchange(n).start()

        @pl.when(n > 0)
        def _():
            finish(n - 1)

        return carry

    lax.fori_loop(0, chunks, gate_up, 0)

    for n in range(chunks):
        wd_copy(n).wait()

    def down(c, carry):
        cols = pl.ds(pl.multiple_of(c * width, width), width)
        total = jnp.zeros((tall, width), f32)
        for n in range(chunks - 1):
            total = total + jnp.dot(units[n], wd[n, :, cols], preferred_element_type=f32)
        acc[c] = total
        return carry

    if chunks > 1:
        lax.fori_loop(0, RETURN_CHUNKS, down, 0)
    finish(chunks - 1)

    def give_back(c, offset):
        target, place = peer(offset)
        return pltpu.make_async_remote_copy(
            src_ref=back.at[c, target],
            dst_ref=returned.at[c, me],
            send_sem=back_sem.at[c, offset],
            recv_sem=return_sem.at[c, offset],
            device_id=place,
            device_id_type=pl.DeviceIdType.MESH,
        )

    def last(c, carry):
        cols = pl.ds(pl.multiple_of(c * width, width), width)
        total = jnp.dot(units[chunks - 1], wd[chunks - 1, :, cols], preferred_element_type=f32)
        if chunks > 1:
            total = total + acc[c]
        total = total.astype(bf16)
        stacked = jnp.concatenate(
            [total[:, j * small : (j + 1) * small] for j in range(PIECES)], axis=0
        )
        sorted_out = jnp.dot(perm_back[...], stacked, preferred_element_type=f32).astype(bf16)
        back[c] = sorted_out.reshape(count, PIECES * rows, small)
        for offset in range(1, count):
            give_back(c, offset).start()
        returned[c, me] = back[c, me]
        return carry

    lax.fori_loop(0, RETURN_CHUNKS, last, 0)

    row_at = lax.broadcasted_iota(jnp.int32, (PIECES * rows, HEAD_DIM), 0) & (rows - 1)
    spread = jnp.zeros(row_at.shape, f32)
    first = jnp.full(row_at.shape, -1, jnp.int32)
    second = jnp.full(row_at.shape, -1, jnp.int32)
    for r in range(rows):
        m, i = divmod(r, own)
        spread = jnp.where(row_at == r, logit_ref[m, i, 0] - logit_ref[m, i, 1], spread)
        first = jnp.where(row_at == r, ids_ref[m, i, 0], first)
        second = jnp.where(row_at == r, ids_ref[m, i, 1], second)
    gate_first = jax.nn.sigmoid(spread)
    gate_second = jax.nn.sigmoid(-spread)
    weights = []
    for e in range(EXP_FLIGHT):
        weight = jnp.where(first == e, gate_first, 0.0) + jnp.where(second == e, gate_second, 0.0)
        weights.append(weight[:, :1])

    per_expert = dev_count // EXP_FLIGHT
    for c in range(RETURN_CHUNKS):
        for offset in range(1, count):
            give_back(c, offset).wait_recv()
        for s in range(sub_count):
            mixture = jnp.zeros((PIECES * rows, small), f32)
            for e in range(EXP_FLIGHT):
                expert_sum = jnp.zeros((PIECES * rows, small), f32)
                for b in range(e * per_expert, (e + 1) * per_expert):
                    expert_sum = expert_sum + returned[c, b * sub_count + s].astype(f32)
                mixture = mixture + weights[e] * expert_sum
            for j in range(PIECES):
                start = s * half + c * width + j * small
                cols = slice(start, start + small)
                result[:, cols] = resid[:, cols] + mixture[j * rows : (j + 1) * rows, :]
    for m in range(micro):
        out_ref[m] = result[m * own : (m + 1) * own, :].astype(bf16)

    for offset in range(1, count):
        dispatch(offset).wait_send()
    for n in range(chunks):
        exchange(n).wait_send()
    for c in range(RETURN_CHUNKS):
        for offset in range(1, count):
            give_back(c, offset).wait_send()


def shards(
    hidden_in, queries, key_new, value_new, key_cache, value_cache, cache_length,
    expert_ids, route_logits, norm_gain, w_gate, w_up, w_down,
):
    micro, own, model = hidden_in.shape
    slots = key_cache.shape[2]
    kv_width = key_cache.shape[3]
    dev_count = lax.axis_size("dev")
    sub_count = lax.axis_size("sub")
    count = dev_count * sub_count
    rows = micro * own
    tall = count * rows
    half, hidden = w_gate.shape
    chunk = min(512, hidden)
    chunks = hidden // chunk
    piece = half // PIECES
    width = half // RETURN_CHUNKS
    small = width // PIECES
    lane_rows = PIECES * rows
    vmem = pl.BlockSpec(memory_space=pltpu.VMEM)
    smem = pl.BlockSpec(memory_space=pltpu.SMEM)
    anywhere = pl.BlockSpec(memory_space=pl.ANY)
    dma = pltpu.SemaphoreType.DMA
    return pl.pallas_call(
        functools.partial(layer_kernel, micro, own, dev_count, sub_count, chunk),
        out_shape=jax.ShapeDtypeStruct((micro, own, model), bf16),
        in_specs=[
            vmem, vmem, vmem, vmem, anywhere, anywhere, smem, smem, smem, vmem,
            anywhere, anywhere, anywhere,
        ],
        out_specs=vmem,
        scratch_shapes=[
            pltpu.VMEM((micro, own, slots, kv_width), bf16),
            pltpu.VMEM((micro, own, slots, kv_width), bf16),
            pltpu.VMEM((chunks, half, chunk), bf16),
            pltpu.VMEM((chunks, half, chunk), bf16),
            pltpu.VMEM((chunks, chunk, half), bf16),
            pltpu.VMEM((rows, HEADS, kv_width), f32),
            pltpu.VMEM((KV_HEADS * rows, GROUP * HEAD_DIM), f32),
            pltpu.VMEM((rows, model), f32),
            pltpu.VMEM((sub_count, lane_rows, piece), bf16),
            pltpu.VMEM((count, lane_rows, piece), bf16),
            pltpu.VMEM((count * lane_rows, count * lane_rows), bf16),
            pltpu.VMEM((count * lane_rows, count * lane_rows), bf16),
            pltpu.VMEM((tall, half), bf16),
            pltpu.VMEM((chunks, 2, tall, chunk), f32),
            pltpu.VMEM((chunks, 2, tall, chunk), f32),
            pltpu.VMEM((chunks, tall, chunk), bf16),
            pltpu.VMEM((RETURN_CHUNKS, tall, width), f32),
            pltpu.VMEM((RETURN_CHUNKS, count, lane_rows, small), bf16),
            pltpu.VMEM((RETURN_CHUNKS, count, lane_rows, small), bf16),
            pltpu.VMEM((rows, model), f32),
            dma((2,)),
            dma((chunks,)),
            dma((chunks,)),
            dma((chunks,)),
            dma((count,)),
            dma((count,)),
            dma((chunks,)),
            dma((chunks,)),
            dma((RETURN_CHUNKS, count)),
            dma((RETURN_CHUNKS, count)),
        ],
        compiler_params=pltpu.CompilerParams(
            collective_id=0, has_side_effects=True, vmem_limit_bytes=56 * 2**20
        ),
    )(
        hidden_in, queries, key_new, value_new, key_cache, value_cache, cache_length,
        expert_ids, route_logits, norm_gain.reshape(1, model), w_gate, w_up, w_down,
    )


def solution(mesh):
    return jax.shard_map(
        shards,
        mesh=mesh,
        in_specs=(
            P(None, ("groups", "dev", "sub"), None),
            P(None, ("groups", "dev", "sub"), None),
            P(None, ("groups", "dev", "sub"), None),
            P(None, ("groups", "dev", "sub"), None),
            P(None, ("groups", "dev", "sub"), None, None),
            P(None, ("groups", "dev", "sub"), None, None),
            P(None, ("groups", "dev", "sub")),
            P(None, ("groups", "dev", "sub"), None),
            P(None, ("groups", "dev", "sub"), None),
            P(),
            P("sub", "dev"),
            P("sub", "dev"),
            P("dev", "sub"),
        ),
        out_specs=P(None, ("groups", "dev", "sub"), None),
        check_vma=False,
    )
```

```python
import functools

import jax
import jax.numpy as jnp
from jax import lax
from jax.experimental import pallas as pl
from jax.experimental.pallas import tpu as pltpu
from jax.sharding import PartitionSpec as P

HEADS = 48
KV_HEADS = 8
HEAD_DIM = 128
GROUP = HEADS // KV_HEADS
EXP_FLIGHT = 2
PIECES = 4
CHUNKS = 3

masked_score = -1e30
f32 = jnp.float32
bf16 = jnp.bfloat16


def permutation(devs, subs, rows, per, inverse):
    senders = devs * subs
    size = senders * PIECES * rows
    i = lax.broadcasted_iota(jnp.int32, (size, size), 0)
    c = lax.broadcasted_iota(jnp.int32, (size, size), 1)
    if inverse:
        i, c = c, i
    row_bits = rows.bit_length() - 1
    sender_bits = senders.bit_length() - 1
    sub_bits = subs.bit_length() - 1
    row = i & (rows - 1)
    sender = lax.shift_right_logical(i, row_bits) & (senders - 1)
    piece = lax.shift_right_logical(i, row_bits + sender_bits)
    if inverse:
        dev = lax.shift_right_logical(sender, sub_bits)
        group = lax.shift_right_logical(dev, per.bit_length() - 1)
        sender = ((dev & (per - 1)) * EXP_FLIGHT + group) * subs + (sender & (subs - 1))
    at = sender * (PIECES * rows) + piece * rows + row
    return jnp.where(at == c, 1.0, 0.0).astype(f32).astype(bf16)


def layer_kernel(
    micro, own, dev_count, sub_count, chunk,
    hidden_ref, query_ref, knew_ref, vnew_ref, kcache_ref, vcache_ref, length_ref,
    ids_ref, logit_ref, gain_ref, wg_ref, wu_ref, wd_ref,
    out_ref,
    kbuf, vbuf, wg, wu, wd, qbig, ctx, resid, stage, send, arrived, perm, perm_back,
    x, parts, other, units, acc, back, partial, summed, returned, result,
    kv_sem, wg_sem, wu_sem, wd_sem, far_send, far_recv, pair_send, pair_recv, near_send, near_recv,
    fwd_send, fwd_recv, part_sem, other_sem, scatter_send, scatter_recv,
    home_send, home_recv, away_send, away_recv,
):
    rows = micro * own
    count = dev_count * sub_count
    my_dev = lax.axis_index("dev")
    my_sub = lax.axis_index("sub")
    me = my_dev * sub_count + my_sub
    per = dev_count // EXP_FLIGHT
    my_group = my_dev // per
    my_place = lax.rem(my_dev, per)
    far = lax.rem(my_dev + per, dev_count)
    half = wg.shape[0]
    chunks = wd.shape[0]
    width = half // CHUNKS
    small = width // PIECES
    group_width = GROUP * HEAD_DIM

    kv_copies = [
        pltpu.make_async_copy(kcache_ref, kbuf, kv_sem.at[0]),
        pltpu.make_async_copy(vcache_ref, vbuf, kv_sem.at[1]),
    ]
    for copy in kv_copies:
        copy.start()

    def wg_copy(c):
        at = pl.ds(c * width, width)
        return (
            pltpu.make_async_copy(wg_ref.at[at], wg.at[at], wg_sem.at[c]),
            pltpu.make_async_copy(wu_ref.at[at], wu.at[at], wu_sem.at[c]),
        )

    def wd_copy(n):
        return pltpu.make_async_copy(wd_ref.at[pl.ds(n * chunk, chunk)], wd.at[n], wd_sem.at[n])

    for c in range(CHUNKS):
        for copy in wg_copy(c):
            copy.start(priority=1)
    for n in range(chunks):
        wd_copy(n).start(priority=1)

    def near(offset):
        return my_group * per + lax.rem(my_place + offset, per)

    def push(src, dst, send_sem, recv_sem, dev, sub):
        return pltpu.make_async_remote_copy(
            src_ref=src,
            dst_ref=dst,
            send_sem=send_sem,
            recv_sem=recv_sem,
            device_id={"dev": dev, "sub": sub},
            device_id_type=pl.DeviceIdType.MESH,
        )

    other_sub = 1 - my_sub
    barrier = pltpu.get_barrier_semaphore()
    peers = [(far, t) for t in range(sub_count)] + [(my_dev, other_sub)]
    peers += [(near(o), t) for o in range(1, per) for t in range(sub_count)]
    for dev, sub in peers:
        pl.semaphore_signal(
            barrier, inc=1, device_id={"dev": dev, "sub": sub},
            device_id_type=pl.DeviceIdType.MESH,
        )

    perm[...] = permutation(dev_count, sub_count, rows, per, False)
    perm_back[...] = permutation(dev_count, sub_count, rows, per, True)

    inv_root = 1.0 / HEAD_DIM**0.5
    qbig[...] = jnp.zeros_like(qbig)
    for r in range(rows):
        m, i = divmod(r, own)
        q = query_ref[m].astype(f32)
        for h in range(HEADS):
            k = h // GROUP
            qbig[r, h : h + 1, k * HEAD_DIM : (k + 1) * HEAD_DIM] = q[
                i : i + 1, h * HEAD_DIM : (h + 1) * HEAD_DIM
            ]
    for copy in kv_copies:
        copy.wait()
    slot = lax.broadcasted_iota(jnp.int32, (HEADS, kbuf.shape[2]), 1)
    for r in range(rows):
        m, i = divmod(r, own)
        q = qbig[r]
        scores = lax.dot_general(
            q.astype(bf16), kbuf[m, i], (((1,), (1,)), ((), ())), preferred_element_type=f32
        ) * inv_root
        new_key = knew_ref[m].astype(f32)[i : i + 1]
        new_value = vnew_ref[m].astype(f32)[i : i + 1]
        fresh = jnp.sum(q * new_key, axis=1, keepdims=True) * inv_root
        visible = slot < length_ref[m, i]
        scores = jnp.where(visible, scores, masked_score)
        top = jnp.maximum(jnp.max(scores, axis=1, keepdims=True), fresh)
        exps = jnp.where(visible, jnp.exp(scores - top), 0.0)
        fresh_exp = jnp.exp(fresh - top)
        total = jnp.sum(exps, axis=1, keepdims=True) + fresh_exp
        probs = (exps / total).astype(bf16)
        fresh_probs = (fresh_exp / total).astype(bf16).astype(f32)
        wide = jnp.dot(probs, vbuf[m, i], preferred_element_type=f32) + fresh_probs * new_value
        for h in range(HEADS):
            k, g = divmod(h, GROUP)
            ctx[k * rows + r : k * rows + r + 1, g * HEAD_DIM : (g + 1) * HEAD_DIM] = wide[
                h : h + 1, k * HEAD_DIM : (k + 1) * HEAD_DIM
            ]

    squares = jnp.zeros((rows, 1), f32)
    for k in range(KV_HEADS):
        cols = slice(k * group_width, (k + 1) * group_width)
        for m in range(micro):
            base = k * rows + m * own
            resid[m * own : (m + 1) * own, cols] = (
                hidden_ref[m, :, cols].astype(f32) + ctx[base : base + own, :]
            )
        value = resid[:, cols]
        squares = squares + jnp.sum(value * value, axis=1, keepdims=True)
    inv_rms = lax.rsqrt(squares / (KV_HEADS * group_width) + 1e-05)
    for s in range(sub_count):
        for c in range(CHUNKS):
            for j in range(PIECES):
                start = s * half + c * width + j * small
                cols = slice(start, start + small)
                stage[s, c, j * rows : (j + 1) * rows, :] = (
                    resid[:, cols] * inv_rms * gain_ref[:, cols]
                )
    send[...] = stage[...].astype(bf16)

    pl.semaphore_wait(barrier, len(peers))

    def to_far(c, t):
        return push(
            send.at[t, c], arrived.at[c, me], far_send.at[c, t], far_recv.at[c, my_sub], far, t
        )

    def from_far(c, t):
        return push(
            send.at[t, c], arrived.at[c, me], far_send.at[c, t], far_recv.at[c, t], far, t
        )

    def to_pair(c):
        return push(
            send.at[other_sub, c], arrived.at[c, me], pair_send.at[c], pair_recv.at[c],
            my_dev, other_sub,
        )

    def to_near(c, o, t):
        return push(
            send.at[t, c], arrived.at[c, me], near_send.at[c, o, t], near_recv.at[c, o, my_sub],
            near(o), t,
        )

    def from_near(c, o, t):
        return push(
            send.at[t, c], arrived.at[c, me], near_send.at[c, o, t], near_recv.at[c, o, t],
            near(o), t,
        )

    def hand_on(c, o):
        at = pl.ds(far * sub_count, sub_count)
        return push(
            arrived.at[c, at], arrived.at[c, at], fwd_send.at[c, o], fwd_recv.at[c, o],
            near(o), my_sub,
        )

    for c in range(CHUNKS):
        for t in range(sub_count):
            to_far(c, t).start()
        for o in range(1, per):
            for t in range(sub_count):
                to_near(c, o, t).start()
        to_pair(c).start()
        arrived[c, me] = send[my_sub, c]
    for c in range(CHUNKS):
        for t in range(sub_count):
            from_far(c, t).wait_recv()
        for o in range(1, per):
            hand_on(c, o).start()

    tall = count * rows

    def exchange(n):
        return push(
            parts.at[n], other.at[n], part_sem.at[n], other_sem.at[n], my_dev, other_sub
        )

    def finish(n):
        exchange(n).wait_recv()
        gate = parts[n, 0] + other[n, 0]
        up = parts[n, 1] + other[n, 1]
        units[n] = (jax.nn.silu(gate) * up).astype(bf16)

    for c in range(CHUNKS):
        to_pair(c).wait_recv()
        for o in range(1, per):
            for t in range(sub_count):
                from_near(c, o, t).wait_recv()
            hand_on(c, o).wait_recv()
        grid = arrived[c].reshape(count * PIECES * rows, small)
        sorted_rows = jnp.dot(perm[...], grid, preferred_element_type=f32).astype(bf16)
        for j in range(PIECES):
            x[:, j * small : (j + 1) * small] = sorted_rows[j * tall : (j + 1) * tall]
        for copy in wg_copy(c):
            copy.wait()

        def gate_up(n, carry):
            at = slice(c * width, (c + 1) * width)
            cols = pl.ds(pl.multiple_of(n * chunk, chunk), chunk)
            gate = jnp.dot(x[...], wg[at, cols], preferred_element_type=f32)
            up = jnp.dot(x[...], wu[at, cols], preferred_element_type=f32)
            if c > 0:
                gate = gate + parts[n, 0]
                up = up + parts[n, 1]
            parts[n, 0] = gate
            parts[n, 1] = up
            if c == CHUNKS - 1:
                exchange(n).start()

                @pl.when(n > 0)
                def _():
                    finish(n - 1)

            return carry

        lax.fori_loop(0, chunks, gate_up, 0)

    for n in range(chunks):
        wd_copy(n).wait()

    def down(c, carry):
        cols = pl.ds(pl.multiple_of(c * width, width), width)
        total = jnp.zeros((tall, width), f32)
        for n in range(chunks - 1):
            total = total + jnp.dot(units[n], wd[n, :, cols], preferred_element_type=f32)
        acc[c] = total
        return carry

    if chunks > 1:
        lax.fori_loop(0, CHUNKS, down, 0)
    finish(chunks - 1)

    blocks = EXP_FLIGHT * sub_count

    def scatter(c, o):
        return push(
            back.at[c, pl.ds(lax.rem(my_place + o, per) * blocks, blocks)],
            partial.at[c, o], scatter_send.at[c, o], scatter_recv.at[c, o], near(o), my_sub,
        )

    landing = my_group * sub_count + my_sub

    def go_home(c):
        return push(
            summed.at[c, my_group * sub_count + other_sub], returned.at[c, landing],
            home_send.at[c], home_recv.at[c], my_dev, other_sub,
        )

    def go_away(c, t):
        return push(
            summed.at[c, (1 - my_group) * sub_count + t], returned.at[c, landing],
            away_send.at[c, t], away_recv.at[c, my_sub], far, t,
        )

    def come_away(c, t):
        return push(
            summed.at[c, (1 - my_group) * sub_count + t], returned.at[c, landing],
            away_send.at[c, t], away_recv.at[c, t], far, t,
        )

    def send_sums(c):
        for o in range(1, per):
            scatter(c, o).wait_recv()
        total = back[c, pl.ds(my_place * blocks, blocks)].astype(f32)
        for o in range(1, per):
            total = total + partial[c, o].astype(f32)
        summed[c] = total.astype(bf16)
        for t in range(sub_count):
            go_away(c, t).start()
        go_home(c).start()
        returned[c, landing] = summed[c, landing]

    for c in range(CHUNKS):
        cols = slice(c * width, (c + 1) * width)
        total = jnp.dot(units[chunks - 1], wd[chunks - 1, :, cols], preferred_element_type=f32)
        if chunks > 1:
            total = total + acc[c]
        total = total.astype(bf16)
        stacked = jnp.concatenate(
            [total[:, j * small : (j + 1) * small] for j in range(PIECES)], axis=0
        )
        sorted_out = jnp.dot(perm_back[...], stacked, preferred_element_type=f32).astype(bf16)
        back[c] = sorted_out.reshape(count, PIECES * rows, small)
        for o in range(1, per):
            scatter(c, o).start()
        if c > 0:
            send_sums(c - 1)
    send_sums(CHUNKS - 1)

    row_at = lax.broadcasted_iota(jnp.int32, (PIECES * rows, HEAD_DIM), 0) & (rows - 1)
    spread = jnp.zeros(row_at.shape, f32)
    first = jnp.full(row_at.shape, -1, jnp.int32)
    second = jnp.full(row_at.shape, -1, jnp.int32)
    for r in range(rows):
        m, i = divmod(r, own)
        spread = jnp.where(row_at == r, logit_ref[m, i, 0] - logit_ref[m, i, 1], spread)
        first = jnp.where(row_at == r, ids_ref[m, i, 0], first)
        second = jnp.where(row_at == r, ids_ref[m, i, 1], second)
    gate_first = jax.nn.sigmoid(spread)
    gate_second = jax.nn.sigmoid(-spread)
    weights = []
    for e in range(EXP_FLIGHT):
        weight = jnp.where(first == e, gate_first, 0.0) + jnp.where(second == e, gate_second, 0.0)
        weights.append(weight[:, :1])

    for c in range(CHUNKS):
        go_home(c).wait_recv()
        for t in range(sub_count):
            come_away(c, t).wait_recv()
        for s in range(sub_count):
            mixture = jnp.zeros((PIECES * rows, small), f32)
            for e in range(EXP_FLIGHT):
                mixture = mixture + weights[e] * returned[c, e * sub_count + s].astype(f32)
            for j in range(PIECES):
                start = s * half + c * width + j * small
                cols = slice(start, start + small)
                result[:, cols] = resid[:, cols] + mixture[j * rows : (j + 1) * rows, :]
    for m in range(micro):
        out_ref[m] = result[m * own : (m + 1) * own, :].astype(bf16)

    for n in range(chunks):
        exchange(n).wait_send()
    for c in range(CHUNKS):
        to_pair(c).wait_send()
        go_home(c).wait_send()
        for t in range(sub_count):
            to_far(c, t).wait_send()
            go_away(c, t).wait_send()
        for o in range(1, per):
            hand_on(c, o).wait_send()
            scatter(c, o).wait_send()
            for t in range(sub_count):
                to_near(c, o, t).wait_send()


def shards(
    hidden_in, queries, key_new, value_new, key_cache, value_cache, cache_length,
    expert_ids, route_logits, norm_gain, w_gate, w_up, w_down,
):
    micro, own, model = hidden_in.shape
    slots = key_cache.shape[2]
    kv_width = key_cache.shape[3]
    dev_count = lax.axis_size("dev")
    sub_count = lax.axis_size("sub")
    count = dev_count * sub_count
    rows = micro * own
    tall = count * rows
    half, hidden = w_gate.shape
    chunk = min(512, hidden)
    chunks = hidden // chunk
    per = dev_count // EXP_FLIGHT
    blocks = EXP_FLIGHT * sub_count
    width = half // CHUNKS
    small = width // PIECES
    lane_rows = PIECES * rows
    vmem = pl.BlockSpec(memory_space=pltpu.VMEM)
    smem = pl.BlockSpec(memory_space=pltpu.SMEM)
    anywhere = pl.BlockSpec(memory_space=pl.ANY)
    dma = pltpu.SemaphoreType.DMA
    return pl.pallas_call(
        functools.partial(layer_kernel, micro, own, dev_count, sub_count, chunk),
        out_shape=jax.ShapeDtypeStruct((micro, own, model), bf16),
        in_specs=[
            vmem, vmem, vmem, vmem, anywhere, anywhere, smem, smem, smem, vmem,
            anywhere, anywhere, anywhere,
        ],
        out_specs=vmem,
        scratch_shapes=[
            pltpu.VMEM((micro, own, slots, kv_width), bf16),
            pltpu.VMEM((micro, own, slots, kv_width), bf16),
            pltpu.VMEM((half, hidden), bf16),
            pltpu.VMEM((half, hidden), bf16),
            pltpu.VMEM((chunks, chunk, half), bf16),
            pltpu.VMEM((rows, HEADS, kv_width), f32),
            pltpu.VMEM((KV_HEADS * rows, GROUP * HEAD_DIM), f32),
            pltpu.VMEM((rows, model), f32),
            pltpu.VMEM((sub_count, CHUNKS, lane_rows, small), f32),
            pltpu.VMEM((sub_count, CHUNKS, lane_rows, small), bf16),
            pltpu.VMEM((CHUNKS, count, lane_rows, small), bf16),
            pltpu.VMEM((count * lane_rows, count * lane_rows), bf16),
            pltpu.VMEM((count * lane_rows, count * lane_rows), bf16),
            pltpu.VMEM((tall, width), bf16),
            pltpu.VMEM((chunks, 2, tall, chunk), f32),
            pltpu.VMEM((chunks, 2, tall, chunk), f32),
            pltpu.VMEM((chunks, tall, chunk), bf16),
            pltpu.VMEM((CHUNKS, tall, width), f32),
            pltpu.VMEM((CHUNKS, count, lane_rows, small), bf16),
            pltpu.VMEM((CHUNKS, per, blocks, lane_rows, small), bf16),
            pltpu.VMEM((CHUNKS, blocks, lane_rows, small), bf16),
            pltpu.VMEM((CHUNKS, blocks, lane_rows, small), bf16),
            pltpu.VMEM((rows, model), f32),
            dma((2,)),
            dma((CHUNKS,)),
            dma((CHUNKS,)),
            dma((chunks,)),
            dma((CHUNKS, sub_count)),
            dma((CHUNKS, sub_count)),
            dma((CHUNKS,)),
            dma((CHUNKS,)),
            dma((CHUNKS, per, sub_count)),
            dma((CHUNKS, per, sub_count)),
            dma((CHUNKS, per)),
            dma((CHUNKS, per)),
            dma((chunks,)),
            dma((chunks,)),
            dma((CHUNKS, per)),
            dma((CHUNKS, per)),
            dma((CHUNKS,)),
            dma((CHUNKS,)),
            dma((CHUNKS, sub_count)),
            dma((CHUNKS, sub_count)),
        ],
        compiler_params=pltpu.CompilerParams(
            collective_id=0, has_side_effects=True, vmem_limit_bytes=56 * 2**20
        ),
    )(
        hidden_in, queries, key_new, value_new, key_cache, value_cache, cache_length,
        expert_ids, route_logits, norm_gain.reshape(1, model), w_gate, w_up, w_down,
    )


def solution(mesh):
    return jax.shard_map(
        shards,
        mesh=mesh,
        in_specs=(
            P(None, ("groups", "dev", "sub"), None),
            P(None, ("groups", "dev", "sub"), None),
            P(None, ("groups", "dev", "sub"), None),
            P(None, ("groups", "dev", "sub"), None),
            P(None, ("groups", "dev", "sub"), None, None),
            P(None, ("groups", "dev", "sub"), None, None),
            P(None, ("groups", "dev", "sub")),
            P(None, ("groups", "dev", "sub"), None),
            P(None, ("groups", "dev", "sub"), None),
            P(),
            P("sub", "dev"),
            P("sub", "dev"),
            P("dev", "sub"),
        ),
        out_specs=P(None, ("groups", "dev", "sub"), None),
        check_vma=False,
    )
```

```python
import functools

import jax
import jax.numpy as jnp
from jax import lax
from jax.experimental import pallas as pl
from jax.experimental.pallas import tpu as pltpu
from jax.sharding import PartitionSpec as P

HEADS = 48
KV_HEADS = 8
HEAD_DIM = 128
GROUP = HEADS // KV_HEADS
EXP_FLIGHT = 2
PIECES = 4
RETURN_CHUNKS = 1

masked_score = -1e30
f32 = jnp.float32
bf16 = jnp.bfloat16


def permutation(senders, rows, inverse):
    size = senders * PIECES * rows
    i = lax.broadcasted_iota(jnp.int32, (size, size), 0)
    c = lax.broadcasted_iota(jnp.int32, (size, size), 1)
    if inverse:
        i, c = c, i
    row_bits = rows.bit_length() - 1
    sender_bits = senders.bit_length() - 1
    row = i & (rows - 1)
    sender = lax.shift_right_logical(i, row_bits) & (senders - 1)
    piece = lax.shift_right_logical(i, row_bits + sender_bits)
    at = sender * (PIECES * rows) + piece * rows + row
    return jnp.where(at == c, 1.0, 0.0).astype(f32).astype(bf16)


def layer_kernel(
    micro, own, dev_count, sub_count, chunk,
    hidden_ref, query_ref, knew_ref, vnew_ref, kcache_ref, vcache_ref, length_ref,
    ids_ref, logit_ref, gain_ref, wg_ref, wu_ref, wd_ref,
    out_ref,
    kbuf, vbuf, wg, wu, wd, qbig, ctx, resid, send, arrived, perm, perm_back,
    x, parts, other, units, acc, back, returned, result,
    kv_sem, wg_sem, wu_sem, wd_sem, send_sem, arrive_sem, part_sem, other_sem, back_sem, return_sem,
):
    rows = micro * own
    count = dev_count * sub_count
    my_dev = lax.axis_index("dev")
    my_sub = lax.axis_index("sub")
    me = my_dev * sub_count + my_sub
    half = wg.shape[1]
    piece = half // PIECES
    chunks = wg.shape[0]
    width = half // RETURN_CHUNKS
    small = width // PIECES
    group_width = GROUP * HEAD_DIM

    kv_copies = [
        pltpu.make_async_copy(kcache_ref, kbuf, kv_sem.at[0]),
        pltpu.make_async_copy(vcache_ref, vbuf, kv_sem.at[1]),
    ]
    for copy in kv_copies:
        copy.start()

    def wg_copy(n):
        cols = pl.ds(pl.multiple_of(n * chunk, chunk), chunk)
        return (
            pltpu.make_async_copy(wg_ref.at[:, cols], wg.at[n], wg_sem.at[n]),
            pltpu.make_async_copy(wu_ref.at[:, cols], wu.at[n], wu_sem.at[n]),
        )

    def wd_copy(n):
        return pltpu.make_async_copy(wd_ref.at[pl.ds(n * chunk, chunk)], wd.at[n], wd_sem.at[n])

    for n in range(chunks):
        for copy in wg_copy(n):
            copy.start(priority=1)
    for n in range(chunks):
        wd_copy(n).start(priority=1)

    def peer(offset):
        target = lax.rem(me + offset, count)
        return target, {"dev": target // sub_count, "sub": lax.rem(target, sub_count)}

    barrier = pltpu.get_barrier_semaphore()
    for offset in range(1, count):
        pl.semaphore_signal(
            barrier, inc=1, device_id=peer(offset)[1], device_id_type=pl.DeviceIdType.MESH
        )

    perm[...] = permutation(count, rows, False)
    perm_back[...] = permutation(count, rows, True)

    inv_root = 1.0 / HEAD_DIM**0.5
    qbig[...] = jnp.zeros_like(qbig)
    for r in range(rows):
        m, i = divmod(r, own)
        q = query_ref[m].astype(f32)
        for h in range(HEADS):
            k = h // GROUP
            qbig[r, h : h + 1, k * HEAD_DIM : (k + 1) * HEAD_DIM] = q[
                i : i + 1, h * HEAD_DIM : (h + 1) * HEAD_DIM
            ]
    for copy in kv_copies:
        copy.wait()
    slot = lax.broadcasted_iota(jnp.int32, (HEADS, kbuf.shape[2]), 1)
    for r in range(rows):
        m, i = divmod(r, own)
        q = qbig[r]
        scores = lax.dot_general(
            q.astype(bf16), kbuf[m, i], (((1,), (1,)), ((), ())), preferred_element_type=f32
        ) * inv_root
        new_key = knew_ref[m].astype(f32)[i : i + 1]
        new_value = vnew_ref[m].astype(f32)[i : i + 1]
        fresh = jnp.sum(q * new_key, axis=1, keepdims=True) * inv_root
        visible = slot < length_ref[m, i]
        scores = jnp.where(visible, scores, masked_score)
        top = jnp.maximum(jnp.max(scores, axis=1, keepdims=True), fresh)
        exps = jnp.where(visible, jnp.exp(scores - top), 0.0)
        fresh_exp = jnp.exp(fresh - top)
        total = jnp.sum(exps, axis=1, keepdims=True) + fresh_exp
        probs = (exps / total).astype(bf16)
        fresh_probs = (fresh_exp / total).astype(bf16).astype(f32)
        wide = jnp.dot(probs, vbuf[m, i], preferred_element_type=f32) + fresh_probs * new_value
        for h in range(HEADS):
            k, g = divmod(h, GROUP)
            ctx[k * rows + r : k * rows + r + 1, g * HEAD_DIM : (g + 1) * HEAD_DIM] = wide[
                h : h + 1, k * HEAD_DIM : (k + 1) * HEAD_DIM
            ]

    squares = jnp.zeros((rows, 1), f32)
    for k in range(KV_HEADS):
        cols = slice(k * group_width, (k + 1) * group_width)
        for m in range(micro):
            base = k * rows + m * own
            resid[m * own : (m + 1) * own, cols] = (
                hidden_ref[m, :, cols].astype(f32) + ctx[base : base + own, :]
            )
        value = resid[:, cols]
        squares = squares + jnp.sum(value * value, axis=1, keepdims=True)
    inv_rms = lax.rsqrt(squares / (KV_HEADS * group_width) + 1e-05)
    for k in range(KV_HEADS):
        cols = slice(k * group_width, (k + 1) * group_width)
        ctx[k * rows : (k + 1) * rows, :] = resid[:, cols] * inv_rms * gain_ref[:, cols]
    for s in range(sub_count):
        send[s] = ctx[s * PIECES * rows : (s + 1) * PIECES * rows, :].astype(bf16)

    pl.semaphore_wait(barrier, count - 1)

    def dispatch(offset):
        target, place = peer(offset)
        return pltpu.make_async_remote_copy(
            src_ref=send.at[lax.rem(target, sub_count)],
            dst_ref=arrived.at[me],
            send_sem=send_sem.at[offset],
            recv_sem=arrive_sem.at[offset],
            device_id=place,
            device_id_type=pl.DeviceIdType.MESH,
        )

    for offset in range(1, count):
        dispatch(offset).start()
    arrived[me] = send[my_sub]
    for offset in range(1, count):
        dispatch(offset).wait_recv()

    grid = arrived[...].reshape(count * PIECES * rows, piece)
    sorted_rows = jnp.dot(perm[...], grid, preferred_element_type=f32).astype(bf16)
    tall = count * rows
    for j in range(PIECES):
        x[:, j * piece : (j + 1) * piece] = sorted_rows[j * tall : (j + 1) * tall]

    def exchange(n):
        return pltpu.make_async_remote_copy(
            src_ref=parts.at[n],
            dst_ref=other.at[n],
            send_sem=part_sem.at[n],
            recv_sem=other_sem.at[n],
            device_id={"dev": my_dev, "sub": 1 - my_sub},
            device_id_type=pl.DeviceIdType.MESH,
        )

    def finish(n):
        exchange(n).wait_recv()
        gate = parts[n, 0] + other[n, 0]
        up = parts[n, 1] + other[n, 1]
        units[n] = (jax.nn.silu(gate) * up).astype(bf16)

    def gate_up(n, carry):
        for copy in wg_copy(n):
            copy.wait()
        parts[n, 0] = jnp.dot(x[...], wg[n], preferred_element_type=f32)
        parts[n, 1] = jnp.dot(x[...], wu[n], preferred_element_type=f32)
        exchange(n).start()

        @pl.when(n > 0)
        def _():
            finish(n - 1)

        return carry

    lax.fori_loop(0, chunks, gate_up, 0)

    for n in range(chunks):
        wd_copy(n).wait()

    def down(c, carry):
        cols = pl.ds(pl.multiple_of(c * width, width), width)
        total = jnp.zeros((tall, width), f32)
        for n in range(chunks - 1):
            total = total + jnp.dot(units[n], wd[n, :, cols], preferred_element_type=f32)
        acc[c] = total
        return carry

    if chunks > 1:
        lax.fori_loop(0, RETURN_CHUNKS, down, 0)
    finish(chunks - 1)

    def give_back(c, offset):
        target, place = peer(offset)
        return pltpu.make_async_remote_copy(
            src_ref=back.at[c, target],
            dst_ref=returned.at[c, me],
            send_sem=back_sem.at[c, offset],
            recv_sem=return_sem.at[c, offset],
            device_id=place,
            device_id_type=pl.DeviceIdType.MESH,
        )

    def last(c, carry):
        cols = pl.ds(pl.multiple_of(c * width, width), width)
        total = jnp.dot(units[chunks - 1], wd[chunks - 1, :, cols], preferred_element_type=f32)
        if chunks > 1:
            total = total + acc[c]
        total = total.astype(bf16)
        stacked = jnp.concatenate(
            [total[:, j * small : (j + 1) * small] for j in range(PIECES)], axis=0
        )
        sorted_out = jnp.dot(perm_back[...], stacked, preferred_element_type=f32).astype(bf16)
        back[c] = sorted_out.reshape(count, PIECES * rows, small)
        for offset in range(1, count):
            give_back(c, offset).start()
        returned[c, me] = back[c, me]
        return carry

    lax.fori_loop(0, RETURN_CHUNKS, last, 0)

    row_at = lax.broadcasted_iota(jnp.int32, (PIECES * rows, HEAD_DIM), 0) & (rows - 1)
    spread = jnp.zeros(row_at.shape, f32)
    first = jnp.full(row_at.shape, -1, jnp.int32)
    second = jnp.full(row_at.shape, -1, jnp.int32)
    for r in range(rows):
        m, i = divmod(r, own)
        spread = jnp.where(row_at == r, logit_ref[m, i, 0] - logit_ref[m, i, 1], spread)
        first = jnp.where(row_at == r, ids_ref[m, i, 0], first)
        second = jnp.where(row_at == r, ids_ref[m, i, 1], second)
    gate_first = jax.nn.sigmoid(spread)
    gate_second = jax.nn.sigmoid(-spread)
    weights = []
    for e in range(EXP_FLIGHT):
        weight = jnp.where(first == e, gate_first, 0.0) + jnp.where(second == e, gate_second, 0.0)
        weights.append(weight[:, :1])

    per_expert = dev_count // EXP_FLIGHT
    for c in range(RETURN_CHUNKS):
        for offset in range(1, count):
            give_back(c, offset).wait_recv()
        for s in range(sub_count):
            mixture = jnp.zeros((PIECES * rows, small), f32)
            for e in range(EXP_FLIGHT):
                expert_sum = jnp.zeros((PIECES * rows, small), f32)
                for b in range(e * per_expert, (e + 1) * per_expert):
                    expert_sum = expert_sum + returned[c, b * sub_count + s].astype(f32)
                mixture = mixture + weights[e] * expert_sum
            for j in range(PIECES):
                start = s * half + c * width + j * small
                cols = slice(start, start + small)
                result[:, cols] = resid[:, cols] + mixture[j * rows : (j + 1) * rows, :]
    for m in range(micro):
        out_ref[m] = result[m * own : (m + 1) * own, :].astype(bf16)

    for offset in range(1, count):
        dispatch(offset).wait_send()
    for n in range(chunks):
        exchange(n).wait_send()
    for c in range(RETURN_CHUNKS):
        for offset in range(1, count):
            give_back(c, offset).wait_send()


def shards(
    hidden_in, queries, key_new, value_new, key_cache, value_cache, cache_length,
    expert_ids, route_logits, norm_gain, w_gate, w_up, w_down,
):
    micro, own, model = hidden_in.shape
    slots = key_cache.shape[2]
    kv_width = key_cache.shape[3]
    dev_count = lax.axis_size("dev")
    sub_count = lax.axis_size("sub")
    count = dev_count * sub_count
    rows = micro * own
    tall = count * rows
    half, hidden = w_gate.shape
    chunk = min(512, hidden)
    chunks = hidden // chunk
    piece = half // PIECES
    width = half // RETURN_CHUNKS
    small = width // PIECES
    lane_rows = PIECES * rows
    vmem = pl.BlockSpec(memory_space=pltpu.VMEM)
    smem = pl.BlockSpec(memory_space=pltpu.SMEM)
    anywhere = pl.BlockSpec(memory_space=pl.ANY)
    dma = pltpu.SemaphoreType.DMA
    return pl.pallas_call(
        functools.partial(layer_kernel, micro, own, dev_count, sub_count, chunk),
        out_shape=jax.ShapeDtypeStruct((micro, own, model), bf16),
        in_specs=[
            vmem, vmem, vmem, vmem, anywhere, anywhere, smem, smem, smem, vmem,
            anywhere, anywhere, anywhere,
        ],
        out_specs=vmem,
        scratch_shapes=[
            pltpu.VMEM((micro, own, slots, kv_width), bf16),
            pltpu.VMEM((micro, own, slots, kv_width), bf16),
            pltpu.VMEM((chunks, half, chunk), bf16),
            pltpu.VMEM((chunks, half, chunk), bf16),
            pltpu.VMEM((chunks, chunk, half), bf16),
            pltpu.VMEM((rows, HEADS, kv_width), f32),
            pltpu.VMEM((KV_HEADS * rows, GROUP * HEAD_DIM), f32),
            pltpu.VMEM((rows, model), f32),
            pltpu.VMEM((sub_count, lane_rows, piece), bf16),
            pltpu.VMEM((count, lane_rows, piece), bf16),
            pltpu.VMEM((count * lane_rows, count * lane_rows), bf16),
            pltpu.VMEM((count * lane_rows, count * lane_rows), bf16),
            pltpu.VMEM((tall, half), bf16),
            pltpu.VMEM((chunks, 2, tall, chunk), f32),
            pltpu.VMEM((chunks, 2, tall, chunk), f32),
            pltpu.VMEM((chunks, tall, chunk), bf16),
            pltpu.VMEM((RETURN_CHUNKS, tall, width), f32),
            pltpu.VMEM((RETURN_CHUNKS, count, lane_rows, small), bf16),
            pltpu.VMEM((RETURN_CHUNKS, count, lane_rows, small), bf16),
            pltpu.VMEM((rows, model), f32),
            dma((2,)),
            dma((chunks,)),
            dma((chunks,)),
            dma((chunks,)),
            dma((count,)),
            dma((count,)),
            dma((chunks,)),
            dma((chunks,)),
            dma((RETURN_CHUNKS, count)),
            dma((RETURN_CHUNKS, count)),
        ],
        compiler_params=pltpu.CompilerParams(
            collective_id=0, has_side_effects=True, vmem_limit_bytes=56 * 2**20
        ),
    )(
        hidden_in, queries, key_new, value_new, key_cache, value_cache, cache_length,
        expert_ids, route_logits, norm_gain.reshape(1, model), w_gate, w_up, w_down,
    )


def solution(mesh):
    return jax.shard_map(
        shards,
        mesh=mesh,
        in_specs=(
            P(None, ("groups", "dev", "sub"), None),
            P(None, ("groups", "dev", "sub"), None),
            P(None, ("groups", "dev", "sub"), None),
            P(None, ("groups", "dev", "sub"), None),
            P(None, ("groups", "dev", "sub"), None, None),
            P(None, ("groups", "dev", "sub"), None, None),
            P(None, ("groups", "dev", "sub")),
            P(None, ("groups", "dev", "sub"), None),
            P(None, ("groups", "dev", "sub"), None),
            P(),
            P("sub", "dev"),
            P("sub", "dev"),
            P("dev", "sub"),
        ),
        out_specs=P(None, ("groups", "dev", "sub"), None),
        check_vma=False,
    )
```
